128 devices in a mesh: sec: 4 (over z), dev: 32 (over x, y, core).
Axes of the slice: x: 4, y: 4, z: 4, core: 2. Of those that a mesh axis runs over, the one named last changes fastest.
Arguments:
- queries: bfloat16 [256, 128, 576], P(('sec', 'dev')), may hold values from -480 to 480
- latent_cache: bfloat16 [256, 1024, 576], P(('sec', 'dev')), may hold values from -4 to 4
- cache_lengths: int32 [256], P(('sec', 'dev')), may hold values from 2 to 1024, as said below
- expert_input: bfloat16 [1024, 7168], P(('sec', 'dev')), may hold values from -6 to 6
- expert_ids: int32 [1024, 8], P(('sec', 'dev')), may hold values from 0 to 31, all different within a row; in each aligned block of 8 rows (0 to 7, 8 to 15, ...) at most 3 rows name the same one
- route_gates: bfloat16 [1024, 8], P(('sec', 'dev')), may hold values from 0.099609375 to 1
- gate_weight: bfloat16 [7168, 65536], P(None, ('sec', 'dev')), may hold values from -0.0625 to 0.0625
- up_weight: bfloat16 [7168, 65536], P(None, ('sec', 'dev')), may hold values from -0.0625 to 0.0625
- down_weight: bfloat16 [65536, 7168], P(('sec', 'dev')), may hold values from -0.125 to 0.125
Outputs:
- context: bfloat16 [256, 128, 512], P(('sec', 'dev'))
- expert_output: bfloat16 [1024, 7168], P(('sec', 'dev'))
The draws below stay inside these ranges and needn't reach their ends.
Inputs may be any that keep to these rules, and one draw needn't show every extreme that they name: `cache_lengths`: the first of each device's 2 rows sees all 1024 positions. `expert_ids`: each row names 8 different experts. Among the rows of one device no expert is named by more than 3 rows, and in every draw some expert is named by exactly 3 rows of some device.
All inputs are finite; a program needn't handle non-finite values.
Results may differ from the reference program's by a relative error of at most 0.005.
Values may be sent and summed in bfloat16 or wider, within the bound.
No kernel may reach another device: no remote copies, remote signals or barrier semaphores. Data moves between devices by JAX's collectives and lax.ppermute only.
A program may use at most 128 MiB of HBM per device.

```python
import math
import jax
import jax.numpy as jnp
import numpy as np
from jax import lax

D = 7168
FF = 2048
HEADS = 128
LAT = 512
ROPE = 64
NOPE = 128
EXPERTS = 32
TOP = 8
CTX = 1024
ROW_ATT = 2
ROW_MOE = 8
CAP = 3
ROWS_ATT = 256
ROWS_MOE = 1024


def first_rope(key):
    return jnp.clip(jax.random.normal(key, (ROWS_ATT, ROPE), jnp.float32), -4.0, 4.0)


def draw_latent_cache(key, part):
    anchor = first_rope(key)
    key = jax.random.fold_in(key, 3)
    entries = jnp.clip(jax.random.normal(key, (ROWS_ATT, CTX, LAT + ROPE), jnp.float32), -4.0, 4.0)
    entries = entries.at[:, 0, LAT:].set(anchor)
    return entries.astype(jnp.bfloat16)


def draw_queries(key, part):
    key = jax.random.fold_in(key, 5)
    noise_key = jax.random.fold_in(key, 0)
    query_values = jnp.clip(jax.random.normal(noise_key, (ROWS_ATT, HEADS, LAT + ROPE), jnp.float32), -4.0, 4.0)
    return query_values.astype(jnp.bfloat16)


def draw_cache_lengths(key, part):
    key = jax.random.fold_in(key, 11)
    spread_key, shift_key = jax.random.split(key)
    blocks = ROWS_ATT // ROW_ATT
    drawn = jax.random.randint(spread_key, (blocks, ROW_ATT), 2, CTX + 1)
    shifts = jax.random.randint(shift_key, (blocks, 1), 0, 4)
    shorter = jnp.maximum(jnp.right_shift(drawn, shifts), 2)
    leading = (jnp.arange(ROW_ATT) == 0)[None, :]
    return jnp.where(leading, CTX, shorter).reshape(ROWS_ATT).astype(jnp.int32)


def block_levels(stream_key, extent, pieces, low, high):
    gain = 1.0
    for axis_at, shards_of in pieces:
        heights = jax.random.uniform(jax.random.fold_in(jax.random.fold_in(stream_key, 6), axis_at), (shards_of,), jnp.float32, low / len(pieces), high / len(pieces))
        gain = gain * jnp.repeat(jnp.exp(heights), extent[axis_at] // shards_of).reshape((-1,) + (1,) * (len(extent) - 1 - axis_at))
    return gain


def shared_out(key, own, number, rows, amount, top, limit, skew):
    ranking = jax.random.permutation(key, amount)
    heavy_load, ordinary = load_shares(amount, rows * top, limit, skew, True), load_shares(amount, rows * top, limit, skew, False)
    places = jnp.arange(amount)

    def named(tallies, offset_by):
        used = int((tallies > 0).sum())
        fixed = max(1, used // 4)
        moved = fixed + (places - fixed + offset_by * (used - fixed)) % max(1, amount - fixed)
        return jnp.zeros((amount,), jnp.int32).at[ranking[jnp.where(places < fixed, places, moved)]].set(jnp.asarray(tallies, jnp.int32))

    tallies = jnp.where(number % 4 == 0, named(heavy_load, number // 4), named(ordinary, number - number // 4 - 1))
    mixed = jax.random.permutation(jax.random.fold_in(own, 3), amount)
    donor, receiver = mixed[0:amount // 2 * 2:2], mixed[1:amount // 2 * 2:2]
    room = jnp.minimum(tallies[donor] - 1, limit - tallies[receiver]) // 2
    room = jnp.where((donor == ranking[0]) | (receiver == ranking[0]) | (tallies[receiver] == 0), 0, jnp.maximum(room, 0))
    moved = jax.random.randint(jax.random.fold_in(own, 4), (amount // 2,), 0, 1 << 20) % (room + 1)
    tallies = tallies.at[donor].add(-moved).at[receiver].add(moved)
    items = jnp.searchsorted(jnp.cumsum(tallies), jnp.arange(rows * top), side="right").astype(jnp.int32)
    grid = items.reshape(top, rows).T
    grid = grid[jax.random.permutation(jax.random.fold_in(own, 1), rows)]
    offset_by = jax.random.randint(jax.random.fold_in(own, 2), (rows, 1), 0, top)
    return jnp.take_along_axis(grid, (jnp.arange(top)[None, :] + offset_by) % top, axis=1)


def load_shares(number_of, total, limit, skew, full):
    weights = [(1 << 20) // math.isqrt(standing ** skew) + 1 for standing in range(1, number_of + 1)]
    largest = limit if full else min(limit, max(-(-total // number_of), total * weights[0] // sum(weights)))
    least = 1 if total - largest >= number_of - 1 else 0
    counts, spare = [largest] + [least] * (number_of - 1), total - largest - least * (number_of - 1)
    while spare > 0:
        candidates = [i for i in range(1, number_of) if counts[i] < largest] or [i for i in range(1, number_of) if counts[i] < limit]
        whole, remaining = sum([weights[i] for i in candidates]), spare
        for i in candidates:
            addition = min(limit - counts[i], max(1, remaining * weights[i] // whole), spare)
            counts[i] = counts[i] + addition
            spare = spare - addition
    return np.array(counts)


def noise(own_key, dims, deviation, reach, pieces=(), kind=jnp.bfloat16):
    loudness = block_levels(own_key, dims, pieces, -0.22, 0.18) if pieces else 1.0
    values = jax.random.normal(own_key, dims, jnp.float32) * deviation * loudness
    return jnp.minimum(jnp.maximum(values, -reach), reach).astype(kind)


def setup_inputs(seed: int = 0) -> dict:
    streams_of = jax.random.split(jax.random.key(seed), 10)
    queries = draw_queries(jax.random.fold_in(streams_of[9], 71), 0)
    latent_cache = draw_latent_cache(jax.random.fold_in(streams_of[9], 71), 0)
    cache_lengths = draw_cache_lengths(jax.random.fold_in(streams_of[9], 71), 0)
    expert_input = noise(streams_of[3], (ROWS_MOE, D), 1.0, 6.0, ((0, 128),))
    expert_ids_keys = jax.random.split(jax.random.fold_in(streams_of[4], 1), ROWS_MOE // ROW_MOE)
    expert_ids_turns = jax.random.permutation(jax.random.fold_in(streams_of[4], 3), ROWS_MOE // ROW_MOE)
    expert_ids = jax.vmap(lambda own, number: shared_out(jax.random.fold_in(streams_of[4], 2), own, number, ROW_MOE, EXPERTS, TOP, CAP, 2))(expert_ids_keys, expert_ids_turns).reshape((ROWS_MOE, TOP))
    route_gates = jnp.clip(jnp.exp(math.log(1.0) - 2.306499 * jax.random.uniform(streams_of[5], (ROWS_MOE, TOP), jnp.float32) ** block_levels(streams_of[5], (ROWS_MOE, TOP), ((0, 128),), -0.2, 0.2)), 0.099609375, 1.0).astype(jnp.bfloat16)
    gate_weight = noise(streams_of[6], (D, EXPERTS * FF), D ** -0.5, 0.0625, ((1, 128),))
    up_weight = noise(streams_of[7], (D, EXPERTS * FF), D ** -0.5, 0.0625, ((1, 128),))
    down_weight = noise(streams_of[8], (EXPERTS * FF, D), FF ** -0.5, 0.125, ((0, 128),))
    return dict(queries=queries, latent_cache=latent_cache, cache_lengths=cache_lengths, expert_input=expert_input, expert_ids=expert_ids, route_gates=route_gates, gate_weight=gate_weight, up_weight=up_weight, down_weight=down_weight)


def attend_row(operands):
    query, cache, length = operands
    scores = jnp.dot(query, cache.T, preferred_element_type=jnp.float32) * ((NOPE + ROPE) ** -0.5)
    visible = (jnp.arange(CTX, dtype=jnp.int32) < length)[None, :]
    highest = jnp.max(jnp.where(visible, scores, -jnp.inf), axis=1, keepdims=True)
    powers = jnp.where(visible, jnp.exp(scores - highest), 0.0)
    attention_weights = (powers / jnp.sum(powers, axis=1, keepdims=True)).astype(jnp.bfloat16)
    return jnp.dot(attention_weights, cache[:, :LAT], preferred_element_type=jnp.float32).astype(jnp.bfloat16)


def reference(queries, latent_cache, cache_lengths, expert_input, expert_ids, route_gates, gate_weight, up_weight, down_weight):
    context = lax.map(attend_row, (queries, latent_cache, cache_lengths))

    def add_expert(running, expert_index):
        start = (expert_index * FF).astype(jnp.int32)
        gate_cols = lax.dynamic_slice_in_dim(gate_weight, start, FF, 1)
        up_cols = lax.dynamic_slice_in_dim(up_weight, start, FF, 1)
        down_rows = lax.dynamic_slice_in_dim(down_weight, start, FF, 0)
        gate_part = jnp.dot(expert_input, gate_cols, preferred_element_type=jnp.float32)
        up_part = jnp.dot(expert_input, up_cols, preferred_element_type=jnp.float32)
        hidden = (jax.nn.silu(gate_part) * up_part).astype(jnp.bfloat16)
        produced = jnp.dot(hidden, down_rows, preferred_element_type=jnp.float32)
        row_gate = jnp.sum(jnp.where(expert_ids == expert_index, route_gates.astype(jnp.float32), 0.0), axis=1)
        return running + row_gate[:, None] * produced, None

    running, _ = lax.scan(add_expert, jnp.zeros((ROWS_MOE, D), jnp.float32), jnp.arange(EXPERTS, dtype=jnp.int32))
    return context, running.astype(jnp.bfloat16)
```

```python
import functools

import jax
import jax.numpy as jnp
import numpy as np
from jax import lax
from jax.experimental import pallas as pl
from jax.experimental.pallas import tpu as pltpu
from jax.sharding import Mesh, PartitionSpec as P

LAT = 512
ROPE = 64
NOPE = 128
EXPERTS = 32
TOP = 8
CAP = 3
D = 7168
ROWS = 8
GROUP = 8
PIECE = D // GROUP
META = 128
SLOTS = GROUP * CAP
CELLS = 16
HELD = CELLS * SLOTS
HIDDEN = 512
ALL = ("z", "x", "y", "c")
BF16 = jnp.bfloat16
F32 = jnp.float32


def attention_rows(queries, latent_cache, cache_lengths):
    scores = jnp.einsum(
        "rhq,rjq->rhj", queries, latent_cache, preferred_element_type=F32
    ) * (NOPE + ROPE) ** (-0.5)
    positions = jnp.arange(latent_cache.shape[1], dtype=jnp.int32)
    visible = (positions[None, :] < cache_lengths[:, None])[:, None, :]
    highest = jnp.max(jnp.where(visible, scores, -jnp.inf), axis=2, keepdims=True)
    powers = jnp.where(visible, jnp.exp(scores - highest), 0.0)
    attention_weights = (powers / jnp.sum(powers, axis=2, keepdims=True)).astype(BF16)
    latents = latent_cache[:, :, :LAT]
    return jnp.einsum(
        "rhj,rjl->rhl", attention_weights, latents, preferred_element_type=F32
    ).astype(BF16)


def slot_constants():
    q = np.arange(2 * HELD)
    h, cell, source, place = q // HELD, q % HELD // SLOTS, q % SLOTS // CAP, q % CAP
    expert_of = (cell * 2 + h)[:, None] == np.arange(EXPERTS)[None, :]
    row = np.arange(GROUP * ROWS)
    same = source[:, None] == row[None, :] // ROWS
    wanted = np.where(same, place[:, None], -2)
    earlier = (row[:, None] // ROWS == row[None, :] // ROWS) & (row[None, :] < row[:, None])
    return (
        jnp.asarray(expert_of, BF16),
        jnp.asarray(wanted, F32),
        jnp.asarray(wanted.T, F32),
        jnp.asarray(earlier, BF16),
    )


def dot(a, b, contract=((1,), (0,))):
    return lax.dot_general(a, b, (contract, ((), ())), preferred_element_type=F32)


def select_kernel(rows_ref, expert_ref, wanted_ref, wanted_t_ref, earlier_ref, send_ref, mix_ref):
    meta = rows_ref[:, PIECE:].astype(F32)
    lane = lax.broadcasted_iota(jnp.int32, (GROUP * ROWS, EXPERTS), 1).astype(F32)
    member = jnp.zeros((GROUP * ROWS, EXPERTS), F32)
    gate = jnp.zeros((GROUP * ROWS, EXPERTS), F32)
    for k in range(TOP):
        hit = meta[:, k : k + 1] == lane
        member = member + jnp.where(hit, 1.0, 0.0)
        gate = gate + jnp.where(hit, meta[:, TOP + k : TOP + k + 1], 0.0)
    rank = dot(earlier_ref[...], member.astype(BF16))
    place = jnp.where(member > 0.0, rank, -1.0).astype(BF16)
    expert = expert_ref[...]
    chosen = dot(expert, place, ((1,), (1,))) == wanted_ref[...]
    chosen_t = dot(place, expert, ((1,), (1,))) == wanted_t_ref[...]
    weight = dot(gate.astype(BF16), expert, ((1,), (1,)))
    mix_ref[...] = jnp.where(chosen_t, weight, 0.0).astype(BF16)
    pick = jnp.where(chosen, 1.0, 0.0).astype(BF16)
    values = rows_ref[:, :PIECE]
    for h in range(2):
        picked = dot(pick[h * HELD : (h + 1) * HELD], values).astype(BF16)
        send_ref[h, 0] = picked
        send_ref[h, 1] = picked


def select_rows(rows):
    return pl.pallas_call(
        select_kernel,
        out_shape=(
            jax.ShapeDtypeStruct((2, 2, HELD, PIECE), BF16),
            jax.ShapeDtypeStruct((GROUP * ROWS, 2 * HELD), BF16),
        ),
        compiler_params=pltpu.CompilerParams(vmem_limit_bytes=40 << 20),
        name="select_rows",
    )(rows, *slot_constants())


def gate_up_kernel(core_ref, got_ref, gate_ref, up_ref, gate_sum_ref, up_sum_ref):
    step = pl.program_id(0)

    @pl.when(step == 0)
    def _():
        gate_sum_ref[...] = jnp.zeros_like(gate_sum_ref)
        up_sum_ref[...] = jnp.zeros_like(up_sum_ref)

    got = got_ref[0]
    gate_sum_ref[...] += dot(got, gate_ref[...])
    up_sum_ref[...] += dot(got, up_ref[...])


def gate_up_first(core, got, gate_weight, up_weight):
    weight_spec = pl.BlockSpec((PIECE, HIDDEN), lambda y, core: (core[0] * 4 + y, 0))
    sum_spec = pl.BlockSpec((HELD, HIDDEN), lambda y, core: (0, 0))
    return pl.pallas_call(
        gate_up_kernel,
        grid_spec=pltpu.PrefetchScalarGridSpec(
            num_scalar_prefetch=1,
            grid=(4,),
            in_specs=[
                pl.BlockSpec((1, HELD, PIECE), lambda y, core: (y, 0, 0)),
                weight_spec,
                weight_spec,
            ],
            out_specs=(sum_spec, sum_spec),
        ),
        out_shape=(jax.ShapeDtypeStruct((HELD, HIDDEN), F32),) * 2,
        compiler_params=pltpu.CompilerParams(vmem_limit_bytes=40 << 20),
        cost_estimate=pl.CostEstimate(
            flops=4 * HELD * HIDDEN * D // 2, bytes_accessed=2 * HIDDEN * D * 2, transcendentals=0
        ),
        name="gate_up_first",
    )(core, got, gate_weight, up_weight)


def hidden_kernel(
    core_ref, got_ref, gate_ref, up_ref, gate_part_ref, up_part_ref, hidden_ref, gate_sum, up_sum
):
    step = pl.program_id(0)

    @pl.when(step == 0)
    def _():
        gate_sum[...] = gate_part_ref[...]
        up_sum[...] = up_part_ref[...]

    got = got_ref[0]
    gate_sum[...] += dot(got, gate_ref[...])
    up_sum[...] += dot(got, up_ref[...])

    @pl.when(step == 3)
    def _():
        hidden_ref[...] = (jax.nn.silu(gate_sum[...]) * up_sum[...]).astype(BF16)


def hidden_rows(core, got, gate_weight, up_weight, gate_part, up_part):
    weight_spec = pl.BlockSpec((PIECE, HIDDEN), lambda y, core: ((1 - core[0]) * 4 + y, 0))
    sum_spec = pl.BlockSpec((HELD, HIDDEN), lambda y, core: (0, 0))
    return pl.pallas_call(
        hidden_kernel,
        grid_spec=pltpu.PrefetchScalarGridSpec(
            num_scalar_prefetch=1,
            grid=(4,),
            in_specs=[
                pl.BlockSpec((1, HELD, PIECE), lambda y, core: (y, 0, 0)),
                weight_spec,
                weight_spec,
                sum_spec,
                sum_spec,
            ],
            out_specs=sum_spec,
            scratch_shapes=[pltpu.VMEM((HELD, HIDDEN), F32)] * 2,
        ),
        out_shape=jax.ShapeDtypeStruct((HELD, HIDDEN), BF16),
        compiler_params=pltpu.CompilerParams(vmem_limit_bytes=40 << 20),
        cost_estimate=pl.CostEstimate(
            flops=4 * HELD * HIDDEN * D // 2, bytes_accessed=2 * HIDDEN * D * 2, transcendentals=0
        ),
        name="hidden_rows",
    )(core, got, gate_weight, up_weight, gate_part, up_part)


def down_kernel(core_ref, hidden_ref, down_ref, *refs):
    made = dot(hidden_ref[...], down_ref[...])
    if len(refs) == 2:
        made = made + refs[0][0].astype(F32)
    refs[-1][0] = made.astype(BF16)


def down_rows(core, hidden, down_weight, other=None):
    own = other is not None

    def columns(y, core):
        return (0, (core[0] if own else 1 - core[0]) * 4 + y)

    block = pl.BlockSpec((1, HELD, PIECE), lambda y, core: (y, 0, 0))
    return pl.pallas_call(
        down_kernel,
        grid_spec=pltpu.PrefetchScalarGridSpec(
            num_scalar_prefetch=1,
            grid=(4,),
            in_specs=[
                pl.BlockSpec((HELD, HIDDEN), lambda y, core: (0, 0)),
                pl.BlockSpec((HIDDEN, PIECE), columns),
            ]
            + [block] * own,
            out_specs=block,
        ),
        out_shape=jax.ShapeDtypeStruct((4, HELD, PIECE), BF16),
        compiler_params=pltpu.CompilerParams(vmem_limit_bytes=40 << 20),
        cost_estimate=pl.CostEstimate(
            flops=HELD * HIDDEN * D, bytes_accessed=HIDDEN * D, transcendentals=0
        ),
        name="down_own" if own else "down_partner",
    )(core, hidden, down_weight, *((other,) if own else ()))


def combine_kernel(mix_ref, got_ref, out_ref):
    total = jnp.zeros((GROUP * ROWS, PIECE), F32)
    for y in range(4):
        total = total + dot(mix_ref[:, y // 2 * HELD : (y // 2 + 1) * HELD], got_ref[y])
    out_ref[...] = total.astype(BF16)


def combine_rows(mix, got):
    return pl.pallas_call(
        combine_kernel,
        out_shape=jax.ShapeDtypeStruct((GROUP * ROWS, PIECE), BF16),
        compiler_params=pltpu.CompilerParams(vmem_limit_bytes=40 << 20),
        name="combine_rows",
    )(mix, got)


def exchange(values, axes):
    return lax.all_to_all(values, axes, split_axis=0, concat_axis=0, tiled=True)


def swap_cores(values):
    return lax.ppermute(values, "c", [(0, 1), (1, 0)])


def expert_rows(expert_input, expert_ids, route_gates, gate_weight, up_weight, down_weight):
    core = lax.axis_index("c").reshape(1)
    pieces = jnp.transpose(expert_input.reshape(ROWS, 2, 4, PIECE), (2, 1, 0, 3))
    meta = jnp.concatenate([expert_ids.astype(BF16), route_gates], axis=1)
    meta = jnp.pad(meta, ((0, 0), (0, META - 2 * TOP)))
    meta = jnp.broadcast_to(meta[None], (GROUP, ROWS, META))
    outgoing = jnp.concatenate([pieces.reshape(GROUP, ROWS, PIECE), meta], axis=2)
    shared = exchange(outgoing, ("y", "c")).reshape(GROUP * ROWS, PIECE + META)

    send, mix = select_rows(shared)
    send = send.reshape(4 * CELLS, SLOTS, PIECE)
    got = exchange(send, ("y", "z", "x")).reshape(4, HELD, PIECE)
    got_other = swap_cores(got)
    gate_part, up_part = gate_up_first(core, got, gate_weight, up_weight)
    hidden = hidden_rows(core, got_other, gate_weight, up_weight, gate_part, up_part)
    other = swap_cores(down_rows(core, hidden, down_weight))
    made = down_rows(core, hidden, down_weight, other)
    made = made.reshape(4 * CELLS, SLOTS, PIECE)
    returned = exchange(made, ("y", "z", "x")).reshape(4, HELD, PIECE)

    merged = combine_rows(mix, returned).reshape(GROUP, ROWS, PIECE)
    pieces = exchange(merged, ("y", "c")).reshape(4, 2, ROWS, PIECE)
    return jnp.transpose(pieces, (2, 1, 0, 3)).reshape(ROWS, D)


def per_device(
    queries,
    latent_cache,
    cache_lengths,
    expert_input,
    expert_ids,
    route_gates,
    gate_weight,
    up_weight,
    down_weight,
):
    context = attention_rows(queries, latent_cache, cache_lengths)
    expert_output = expert_rows(
        expert_input, expert_ids, route_gates, gate_weight, up_weight, down_weight
    )
    return (context, expert_output)


def solution(mesh):
    chips = Mesh(mesh.devices.reshape(4, 4, 4, 2), ALL)
    return jax.shard_map(
        per_device,
        mesh=chips,
        in_specs=(
            P(ALL, None, None),
            P(ALL, None, None),
            P(ALL),
            P(ALL, None),
            P(ALL, None),
            P(ALL, None),
            P(None, ALL),
            P(None, ALL),
            P(ALL, None),
        ),
        out_specs=(P(ALL, None, None), P(ALL, None)),
        check_vma=False,
    )
```

```python
import jax
import jax.numpy as jnp
from jax import lax
from jax.experimental import pallas as pl
from jax.experimental.pallas import tpu as pltpu
from jax.sharding import Mesh, PartitionSpec as P

LAT = 512
ROPE = 64
NOPE = 128
EXPERTS = 32
TOP = 8
CAP = 3
D = 7168
HIDDEN = 512
ROWS = 8
FOLD = 8
WIDTH = D // FOLD
CELLS = 16
MESSAGE = CAP * FOLD
SENDERS = 64
SLOTS = SENDERS * CAP
CHUNK = 32
TILE = CHUNK * FOLD
ALL = ("z", "x", "y", "c")
BF16 = jnp.bfloat16
F32 = jnp.float32


def attention_rows(queries, latent_cache, cache_lengths):
    scores = jnp.einsum(
        "rhq,rjq->rhj", queries, latent_cache, preferred_element_type=F32
    ) * (NOPE + ROPE) ** (-0.5)
    positions = jnp.arange(latent_cache.shape[1], dtype=jnp.int32)
    visible = (positions[None, :] < cache_lengths[:, None])[:, None, :]
    highest = jnp.max(jnp.where(visible, scores, -jnp.inf), axis=2, keepdims=True)
    powers = jnp.where(visible, jnp.exp(scores - highest), 0.0)
    attention_weights = (powers / jnp.sum(powers, axis=2, keepdims=True)).astype(BF16)
    latents = latent_cache[:, :, :LAT]
    return jnp.einsum(
        "rhj,rjl->rhl", attention_weights, latents, preferred_element_type=F32
    ).astype(BF16)


def dot(a, b, contract=((1,), (0,))):
    return lax.dot_general(a, b, (contract, ((), ())), preferred_element_type=F32)


def array(*shape, dtype=BF16):
    return jax.ShapeDtypeStruct(shape, dtype)


def in_vmem(count):
    return [pl.BlockSpec(memory_space=pltpu.VMEM)] * count


def in_hbm(count):
    return [pl.BlockSpec(memory_space=pltpu.HBM)] * count


def call(kernel, name, out_shape, *operands, limit=12, scalars=0, hbm=0, **settings):
    many = isinstance(out_shape, tuple)
    return pl.pallas_call(
        kernel,
        in_specs=[pl.BlockSpec(memory_space=pltpu.SMEM)] * scalars
        + in_vmem(len(operands) - scalars - hbm)
        + in_hbm(hbm),
        out_specs=tuple(in_vmem(len(out_shape))) if many else in_vmem(1)[0],
        out_shape=out_shape,
        compiler_params=pltpu.CompilerParams(vmem_limit_bytes=limit << 20),
        name=name,
        **settings,
    )(*operands)


def index_of(shape, axis):
    return lax.broadcasted_iota(jnp.int32, shape, axis).astype(F32)


def quotient(values, divisor):
    return jnp.floor((values + 0.5) * (1.0 / divisor))


def remainder(values, divisor):
    return values - quotient(values, divisor) * divisor


def slot_matches(shape, axis):
    q, p = index_of(shape, axis), index_of(shape, 1 - axis)
    place = quotient(remainder(q, MESSAGE), FOLD)
    same_part = remainder(q, FOLD) == quotient(p, ROWS)
    lanes = (2 * CELLS * MESSAGE, EXPERTS)
    q = index_of(lanes, 0)
    h = quotient(q, CELLS * MESSAGE)
    expert = quotient(q - h * (CELLS * MESSAGE), MESSAGE) * 2 + h
    lanes = jnp.where(expert == index_of(lanes, 1), 1.0, 0.0).astype(BF16)
    return lanes, place, same_part


def select_kernel(input_ref, ids_ref, gates_ref, send_ref, mix_ref):
    ids, gates = ids_ref[...].astype(F32), gates_ref[...].astype(F32)
    lane = index_of((ROWS, EXPERTS), 1)
    member = jnp.zeros(lane.shape, F32)
    gate = jnp.zeros(lane.shape, F32)
    for k in range(TOP):
        hit = ids[:, k : k + 1] == lane
        member = member + jnp.where(hit, 1.0, 0.0)
        gate = gate + jnp.where(hit, gates[:, k : k + 1], 0.0)
    earlier = index_of((ROWS, ROWS), 1) < index_of((ROWS, ROWS), 0)
    rank = dot(jnp.where(earlier, 1.0, 0.0), member)
    place = jnp.where(member > 0.0, rank, -1.0)
    place = jnp.concatenate([place] * FOLD, axis=0).astype(BF16)
    gate = jnp.concatenate([gate] * FOLD, axis=0).astype(BF16)
    folded = jnp.concatenate(
        [input_ref[:, k * WIDTH : (k + 1) * WIDTH] for k in range(FOLD)], axis=0
    )
    half = CELLS * MESSAGE

    lanes, wanted, same_part = slot_matches((2 * half, FOLD * ROWS), 0)
    chosen = (dot(lanes, place, ((1,), (1,))) == wanted) & same_part
    pick = jnp.where(chosen, 1.0, 0.0).astype(BF16)
    for h in range(2):
        picked = dot(pick[h * half : (h + 1) * half], folded).astype(BF16)
        send_ref[h, 0] = picked
        send_ref[h, 1] = picked

    _, wanted, same_part = slot_matches((FOLD * ROWS, 2 * half), 1)
    chosen = (dot(place, lanes, ((1,), (1,))) == wanted) & same_part
    weight = dot(gate, lanes, ((1,), (1,)))
    mix_ref[...] = jnp.where(chosen, weight, 0.0).astype(BF16)


def unfold_kernel(got_ref, rows_ref):
    row, column = index_of((TILE, TILE), 0), index_of((TILE, TILE), 1)
    order = remainder(row, CHUNK) * FOLD + quotient(row, CHUNK) == column
    order = jnp.where(order, 1.0, 0.0).astype(BF16)
    for b in range(SLOTS // CHUNK):
        moved = dot(order, got_ref[b * TILE : (b + 1) * TILE]).astype(BF16)
        for k in range(FOLD):
            rows_ref[b * CHUNK : (b + 1) * CHUNK, k * WIDTH : (k + 1) * WIDTH] = moved[
                k * CHUNK : (k + 1) * CHUNK
            ]


def hidden_kernel(rows_ref, gate_ref, up_ref, hidden_ref):
    gate = dot(rows_ref[...], gate_ref[...])
    up = dot(rows_ref[...], up_ref[...])
    hidden_ref[...] = (jax.nn.silu(gate) * up).astype(BF16)


def down_kernel(own_ref, other_ref, own_down, other_down, made_ref, parts):
    for k in range(FOLD):
        columns = slice(k * WIDTH, (k + 1) * WIDTH)
        made = dot(own_ref[...], own_down[:, columns]) + dot(other_ref[...], other_down[:, columns])
        parts[k] = made.astype(BF16)
    row, column = index_of((TILE, TILE), 0), index_of((TILE, TILE), 1)
    order = remainder(row, FOLD) * CHUNK + quotient(row, FOLD) == column
    order = jnp.where(order, 1.0, 0.0).astype(BF16)
    for b in range(SLOTS // CHUNK):
        rows = [parts[k, b * CHUNK : (b + 1) * CHUNK] for k in range(FOLD)]
        moved = dot(order, jnp.concatenate(rows, axis=0))
        made_ref[b * TILE : (b + 1) * TILE] = moved.astype(BF16)


def combine_kernel(mix_ref, got_ref, out_ref):
    half = CELLS * MESSAGE
    total = jnp.zeros((FOLD * ROWS, WIDTH), F32)
    for y in range(4):
        total = total + dot(mix_ref[:, y // 2 * half : (y // 2 + 1) * half], got_ref[y])
    total = total.astype(BF16)
    for k in range(FOLD):
        out_ref[:, k * WIDTH : (k + 1) * WIDTH] = total[k * ROWS : (k + 1) * ROWS]


def exchange(values):
    values = values.reshape(SENDERS, MESSAGE, WIDTH)
    return lax.all_to_all(values, ("y", "z", "x"), split_axis=0, concat_axis=0, tiled=True)


def swap_cores(values):
    return lax.ppermute(values, "c", [(0, 1), (1, 0)])


def cost(flops, size):
    return pl.CostEstimate(flops=flops, bytes_accessed=size, transcendentals=0)


def expert_rows(
    attention, expert_input, expert_ids, route_gates, gate_weight, up_weight, down_weight
):
    send, mix = call(
        select_kernel, "select",
        (array(2, 2, CELLS * MESSAGE, WIDTH), array(FOLD * ROWS, 2 * CELLS * MESSAGE)),
        expert_input, expert_ids, route_gates,
    )
    got = exchange(send).reshape(SLOTS * FOLD, WIDTH)
    down_other = swap_cores(down_weight)
    rows = call(
        unfold_kernel, "unfold", array(SLOTS, D), got, cost_estimate=cost(8 * 10**9, 4 * SLOTS * D)
    )
    rows_other = swap_cores(rows)
    queries, latent_cache, cache_lengths = attention
    queries, rows = lax.optimization_barrier((queries, rows))
    context = attention_rows(queries, latent_cache, cache_lengths)
    context, rows = lax.optimization_barrier((context, rows))

    flops, size = 4 * SLOTS * D * HIDDEN, 4 * D * HIDDEN
    own, other = (
        call(
            hidden_kernel, "hidden", array(SLOTS, HIDDEN), held, gate_weight, up_weight,
            cost_estimate=cost(flops, size),
        )
        for held in (rows, rows_other)
    )
    made = call(
        down_kernel, "down", array(SLOTS * FOLD, WIDTH),
        own, swap_cores(other), down_weight, down_other, cost_estimate=cost(flops, size),
        scratch_shapes=[pltpu.VMEM((FOLD, SLOTS, WIDTH), BF16)],
    )
    returned = exchange(made).reshape(4, CELLS * MESSAGE, WIDTH)
    return context, call(combine_kernel, "combine", array(ROWS, D), mix, returned)


def per_device(
    queries,
    latent_cache,
    cache_lengths,
    expert_input,
    expert_ids,
    route_gates,
    gate_weight,
    up_weight,
    down_weight,
):
    attention = (queries, latent_cache, cache_lengths)
    return expert_rows(
        attention, expert_input, expert_ids, route_gates, gate_weight, up_weight, down_weight
    )


def solution(mesh):
    chips = Mesh(mesh.devices.reshape(4, 4, 4, 2), ALL)
    return jax.shard_map(
        per_device,
        mesh=chips,
        in_specs=(
            P(ALL, None, None),
            P(ALL, None, None),
            P(ALL),
            P(ALL, None),
            P(ALL, None),
            P(ALL, None),
            P(None, ALL),
            P(None, ALL),
            P(ALL, None),
        ),
        out_specs=(P(ALL, None, None), P(ALL, None)),
        check_vma=False,
    )
```

```python
import jax
import jax.numpy as jnp
from jax import lax
from jax.experimental import pallas as pl
from jax.experimental.pallas import tpu as pltpu
from jax.sharding import Mesh, PartitionSpec as P

LAT = 512
ROPE = 64
NOPE = 128
EXPERTS = 32
TOP = 8
CAP = 3
D = 7168
HIDDEN = 512
ROWS = 8
META = 128
FOLD = 8
WIDTH = D // FOLD
CELLS = 16
MESSAGE = CAP * FOLD
SENDERS = 64
SLOTS = SENDERS * CAP
CHUNK = 32
TILE = CHUNK * FOLD
ALL = ("z", "x", "y", "c")
BF16 = jnp.bfloat16
F32 = jnp.float32


def attention_rows(queries, latent_cache, cache_lengths):
    scores = jnp.einsum(
        "rhq,rjq->rhj", queries, latent_cache, preferred_element_type=F32
    ) * (NOPE + ROPE) ** (-0.5)
    positions = jnp.arange(latent_cache.shape[1], dtype=jnp.int32)
    visible = (positions[None, :] < cache_lengths[:, None])[:, None, :]
    highest = jnp.max(jnp.where(visible, scores, -jnp.inf), axis=2, keepdims=True)
    powers = jnp.where(visible, jnp.exp(scores - highest), 0.0)
    attention_weights = (powers / jnp.sum(powers, axis=2, keepdims=True)).astype(BF16)
    latents = latent_cache[:, :, :LAT]
    return jnp.einsum(
        "rhj,rjl->rhl", attention_weights, latents, preferred_element_type=F32
    ).astype(BF16)


def dot(a, b, contract=((1,), (0,))):
    return lax.dot_general(a, b, (contract, ((), ())), preferred_element_type=F32)


def array(*shape, dtype=BF16):
    return jax.ShapeDtypeStruct(shape, dtype)


def in_vmem(count):
    return [pl.BlockSpec(memory_space=pltpu.VMEM)] * count


def in_hbm(count):
    return [pl.BlockSpec(memory_space=pltpu.HBM)] * count


def call(kernel, name, out_shape, *operands, limit=12, scalars=0, hbm=0, **settings):
    many = isinstance(out_shape, tuple)
    return pl.pallas_call(
        kernel,
        in_specs=[pl.BlockSpec(memory_space=pltpu.SMEM)] * scalars
        + in_vmem(len(operands) - scalars - hbm)
        + in_hbm(hbm),
        out_specs=tuple(in_vmem(len(out_shape))) if many else in_vmem(1)[0],
        out_shape=out_shape,
        compiler_params=pltpu.CompilerParams(vmem_limit_bytes=limit << 20),
        name=name,
        **settings,
    )(*operands)


def index_of(shape, axis):
    return lax.broadcasted_iota(jnp.int32, shape, axis).astype(F32)


def quotient(values, divisor):
    return jnp.floor((values + 0.5) * (1.0 / divisor))


def remainder(values, divisor):
    return values - quotient(values, divisor) * divisor


def slot_matches(shape, axis):
    q, p = index_of(shape, axis), index_of(shape, 1 - axis)
    place = quotient(remainder(q, MESSAGE), FOLD)
    same_part = remainder(q, FOLD) == quotient(p, ROWS)
    lanes = (2 * CELLS * MESSAGE, EXPERTS)
    q = index_of(lanes, 0)
    h = quotient(q, CELLS * MESSAGE)
    expert = quotient(q - h * (CELLS * MESSAGE), MESSAGE) * 2 + h
    lanes = jnp.where(expert == index_of(lanes, 1), 1.0, 0.0).astype(BF16)
    return lanes, place, same_part


def select_kernel(input_ref, send_ref, mix_ref):
    meta = input_ref[:, D:].astype(F32)
    ids, gates = meta[:, :TOP], meta[:, TOP : 2 * TOP]
    lane = index_of((ROWS, EXPERTS), 1)
    member = jnp.zeros(lane.shape, F32)
    gate = jnp.zeros(lane.shape, F32)
    for k in range(TOP):
        hit = ids[:, k : k + 1] == lane
        member = member + jnp.where(hit, 1.0, 0.0)
        gate = gate + jnp.where(hit, gates[:, k : k + 1], 0.0)
    earlier = index_of((ROWS, ROWS), 1) < index_of((ROWS, ROWS), 0)
    rank = dot(jnp.where(earlier, 1.0, 0.0), member)
    place = jnp.where(member > 0.0, rank, -1.0)
    place = jnp.concatenate([place] * FOLD, axis=0).astype(BF16)
    gate = jnp.concatenate([gate] * FOLD, axis=0).astype(BF16)
    folded = jnp.concatenate(
        [input_ref[:, k * WIDTH : (k + 1) * WIDTH] for k in range(FOLD)], axis=0
    )
    half = CELLS * MESSAGE

    lanes, wanted, same_part = slot_matches((2 * half, FOLD * ROWS), 0)
    chosen = (dot(lanes, place, ((1,), (1,))) == wanted) & same_part
    pick = jnp.where(chosen, 1.0, 0.0).astype(BF16)
    for h in range(2):
        picked = dot(pick[h * half : (h + 1) * half], folded).astype(BF16)
        send_ref[h, 0] = picked
        send_ref[h, 1] = picked

    _, wanted, same_part = slot_matches((FOLD * ROWS, 2 * half), 1)
    chosen = (dot(place, lanes, ((1,), (1,))) == wanted) & same_part
    weight = dot(gate, lanes, ((1,), (1,)))
    mix_ref[...] = jnp.where(chosen, weight, 0.0).astype(BF16)


def unfold_kernel(got_ref, rows_ref):
    row, column = index_of((TILE, TILE), 0), index_of((TILE, TILE), 1)
    order = remainder(row, CHUNK) * FOLD + quotient(row, CHUNK) == column
    order = jnp.where(order, 1.0, 0.0).astype(BF16)
    for b in range(SLOTS // CHUNK):
        moved = dot(order, got_ref[b * TILE : (b + 1) * TILE]).astype(BF16)
        for k in range(FOLD):
            rows_ref[b * CHUNK : (b + 1) * CHUNK, k * WIDTH : (k + 1) * WIDTH] = moved[
                k * CHUNK : (k + 1) * CHUNK
            ]


def hidden_kernel(rows_ref, gate_ref, up_ref, hidden_ref):
    gate = dot(rows_ref[...], gate_ref[...])
    up = dot(rows_ref[...], up_ref[...])
    hidden_ref[...] = (jax.nn.silu(gate) * up).astype(BF16)


def down_kernel(own_ref, other_ref, own_down, other_down, made_ref, parts):
    for k in range(0, FOLD, 2):
        columns = slice(k * WIDTH, (k + 2) * WIDTH)
        made = dot(own_ref[...], own_down[:, columns]) + dot(other_ref[...], other_down[:, columns])
        made = made.astype(BF16)
        parts[k], parts[k + 1] = made[:, :WIDTH], made[:, WIDTH:]
    row, column = index_of((TILE, TILE), 0), index_of((TILE, TILE), 1)
    order = remainder(row, FOLD) * CHUNK + quotient(row, FOLD) == column
    order = jnp.where(order, 1.0, 0.0).astype(BF16)
    for b in range(SLOTS // CHUNK):
        rows = [parts[k, b * CHUNK : (b + 1) * CHUNK] for k in range(FOLD)]
        moved = dot(order, jnp.concatenate(rows, axis=0))
        made_ref[b * TILE : (b + 1) * TILE] = moved.astype(BF16)


def combine_kernel(mix_ref, got_ref, out_ref):
    half = CELLS * MESSAGE
    total = jnp.zeros((FOLD * ROWS, WIDTH), F32)
    for y in range(4):
        total = total + dot(mix_ref[:, y // 2 * half : (y // 2 + 1) * half], got_ref[y])
    total = total.astype(BF16)
    for k in range(FOLD):
        out_ref[:, k * WIDTH : (k + 1) * WIDTH] = total[k * ROWS : (k + 1) * ROWS]


def exchange(values):
    values = values.reshape(SENDERS, MESSAGE, WIDTH)
    return lax.all_to_all(values, ("y", "z", "x"), split_axis=0, concat_axis=0, tiled=True)


def swap_cores(values):
    return lax.ppermute(values, "c", [(0, 1), (1, 0)])


def cost(flops, size):
    return pl.CostEstimate(flops=flops, bytes_accessed=size, transcendentals=0)


def expert_rows(
    attention, expert_input, expert_ids, route_gates, gate_weight, up_weight, down_weight
):
    ids = jnp.pad(expert_ids.astype(BF16), ((0, 0), (D, META - TOP)))
    gates = jnp.pad(route_gates, ((0, 0), (D + TOP, META - 2 * TOP)))
    packed = jnp.pad(expert_input, ((0, 0), (0, META)))
    packed = packed + (ids + gates)
    send, mix = call(
        select_kernel, "select",
        (array(2, 2, CELLS * MESSAGE, WIDTH), array(FOLD * ROWS, 2 * CELLS * MESSAGE)),
        packed, cost_estimate=cost(8 * 10**9, 4 * SLOTS * D),
    )
    got = exchange(send).reshape(SLOTS * FOLD, WIDTH)
    down_other = swap_cores(down_weight)
    rows = call(
        unfold_kernel, "unfold", array(SLOTS, D), got, cost_estimate=cost(10**9, 4 * SLOTS * D)
    )
    rows_other = swap_cores(rows)
    queries, latent_cache, cache_lengths = attention
    queries, rows = lax.optimization_barrier((queries, rows))
    context = attention_rows(queries, latent_cache, cache_lengths)

    flops, size = 4 * SLOTS * D * HIDDEN, 4 * D * HIDDEN

    def hidden_rows(held):
        return call(
            hidden_kernel, "hidden", array(SLOTS, HIDDEN), held, gate_weight, up_weight,
            cost_estimate=cost(flops, size),
        )

    own, rows_other = lax.optimization_barrier((hidden_rows(rows), rows_other))
    other = swap_cores(hidden_rows(rows_other))
    context, other = lax.optimization_barrier((context, other))
    made = call(
        down_kernel, "down", array(SLOTS * FOLD, WIDTH),
        own, other, down_weight, down_other, cost_estimate=cost(flops, size),
        scratch_shapes=[pltpu.VMEM((FOLD, SLOTS, WIDTH), BF16)],
    )
    returned = exchange(made).reshape(4, CELLS * MESSAGE, WIDTH)
    return context, call(combine_kernel, "combine", array(ROWS, D), mix, returned)


def per_device(
    queries,
    latent_cache,
    cache_lengths,
    expert_input,
    expert_ids,
    route_gates,
    gate_weight,
    up_weight,
    down_weight,
):
    attention = (queries, latent_cache, cache_lengths)
    return expert_rows(
        attention, expert_input, expert_ids, route_gates, gate_weight, up_weight, down_weight
    )


def solution(mesh):
    chips = Mesh(mesh.devices.reshape(4, 4, 4, 2), ALL)
    return jax.shard_map(
        per_device,
        mesh=chips,
        in_specs=(
            P(ALL, None, None),
            P(ALL, None, None),
            P(ALL),
            P(ALL, None),
            P(ALL, None),
            P(ALL, None),
            P(None, ALL),
            P(None, ALL),
            P(ALL, None),
        ),
        out_specs=(P(ALL, None, None), P(ALL, None)),
        check_vma=False,
    )
```

```python
import jax
import jax.numpy as jnp
from jax import lax
from jax.experimental import pallas as pl
from jax.experimental.pallas import tpu as pltpu
from jax.sharding import Mesh, PartitionSpec as P

LAT = 512
ROPE = 64
NOPE = 128
EXPERTS = 32
TOP = 8
CAP = 3
D = 7168
HIDDEN = 512
ROWS = 8
META = 128
FOLD = 8
WIDTH = D // FOLD
CELLS = 16
MESSAGE = CAP * FOLD
SENDERS = 64
SLOTS = SENDERS * CAP
CHUNK = 32
TILE = CHUNK * FOLD
ALL = "device"
BF16 = jnp.bfloat16
F32 = jnp.float32


def attention_rows(queries, latent_cache, cache_lengths):
    scores = jnp.einsum(
        "rhq,rjq->rhj", queries, latent_cache, preferred_element_type=F32
    ) * (NOPE + ROPE) ** (-0.5)
    positions = jnp.arange(latent_cache.shape[1], dtype=jnp.int32)
    visible = (positions[None, :] < cache_lengths[:, None])[:, None, :]
    highest = jnp.max(jnp.where(visible, scores, -jnp.inf), axis=2, keepdims=True)
    powers = jnp.where(visible, jnp.exp(scores - highest), 0.0)
    attention_weights = (powers / jnp.sum(powers, axis=2, keepdims=True)).astype(BF16)
    latents = latent_cache[:, :, :LAT]
    return jnp.einsum(
        "rhj,rjl->rhl", attention_weights, latents, preferred_element_type=F32
    ).astype(BF16)


def dot(a, b, contract=((1,), (0,))):
    return lax.dot_general(a, b, (contract, ((), ())), preferred_element_type=F32)


def array(*shape, dtype=BF16):
    return jax.ShapeDtypeStruct(shape, dtype)


def in_vmem(count):
    return [pl.BlockSpec(memory_space=pltpu.VMEM)] * count


def in_hbm(count):
    return [pl.BlockSpec(memory_space=pltpu.HBM)] * count


def call(kernel, name, out_shape, *operands, limit=12, scalars=0, hbm=0, **settings):
    many = isinstance(out_shape, tuple)
    return pl.pallas_call(
        kernel,
        in_specs=[pl.BlockSpec(memory_space=pltpu.SMEM)] * scalars
        + in_vmem(len(operands) - scalars - hbm)
        + in_hbm(hbm),
        out_specs=tuple(in_vmem(len(out_shape))) if many else in_vmem(1)[0],
        out_shape=out_shape,
        compiler_params=pltpu.CompilerParams(vmem_limit_bytes=limit << 20),
        name=name,
        **settings,
    )(*operands)


def index_of(shape, axis):
    return lax.broadcasted_iota(jnp.int32, shape, axis).astype(F32)


def quotient(values, divisor):
    return jnp.floor((values + 0.5) * (1.0 / divisor))


def remainder(values, divisor):
    return values - quotient(values, divisor) * divisor


def slot_matches(shape, axis):
    q, p = index_of(shape, axis), index_of(shape, 1 - axis)
    place = quotient(remainder(q, MESSAGE), FOLD)
    same_part = remainder(q, FOLD) == quotient(p, ROWS)
    lanes = (2 * CELLS * MESSAGE, EXPERTS)
    q = index_of(lanes, 0)
    h = quotient(q, CELLS * MESSAGE)
    expert = (EXPERTS - 1) - (quotient(q - h * (CELLS * MESSAGE), MESSAGE) * 2 + h)
    lanes = jnp.where(expert == index_of(lanes, 1), 1.0, 0.0).astype(BF16)
    return lanes, place, same_part


def select_kernel(input_ref, send_ref, mix_ref):
    meta = input_ref[:, D:].astype(F32)
    ids, gates = meta[:, :TOP], meta[:, TOP : 2 * TOP]
    lane = index_of((ROWS, EXPERTS), 1)
    member = jnp.zeros(lane.shape, F32)
    gate = jnp.zeros(lane.shape, F32)
    for k in range(TOP):
        hit = ids[:, k : k + 1] == lane
        member = member + jnp.where(hit, 1.0, 0.0)
        gate = gate + jnp.where(hit, gates[:, k : k + 1], 0.0)
    earlier = index_of((ROWS, ROWS), 1) < index_of((ROWS, ROWS), 0)
    rank = dot(jnp.where(earlier, 1.0, 0.0), member)
    place = jnp.where(member > 0.0, rank, -1.0)
    place = jnp.concatenate([place] * FOLD, axis=0).astype(BF16)
    gate = jnp.concatenate([gate] * FOLD, axis=0).astype(BF16)
    folded = jnp.concatenate(
        [input_ref[:, k * WIDTH : (k + 1) * WIDTH] for k in range(FOLD)], axis=0
    )
    half = CELLS * MESSAGE

    lanes, wanted, same_part = slot_matches((2 * half, FOLD * ROWS), 0)
    chosen = (dot(lanes, place, ((1,), (1,))) == wanted) & same_part
    pick = jnp.where(chosen, 1.0, 0.0).astype(BF16)
    for h in range(2):
        picked = dot(pick[h * half : (h + 1) * half], folded).astype(BF16)
        send_ref[h, 0] = picked
        send_ref[h, 1] = picked

    _, wanted, same_part = slot_matches((FOLD * ROWS, 2 * half), 1)
    chosen = (dot(place, lanes, ((1,), (1,))) == wanted) & same_part
    weight = dot(gate, lanes, ((1,), (1,)))
    mix_ref[...] = jnp.where(chosen, weight, 0.0).astype(BF16)


def unfold_kernel(got_ref, rows_ref):
    row, column = index_of((TILE, TILE), 0), index_of((TILE, TILE), 1)
    order = remainder(row, CHUNK) * FOLD + quotient(row, CHUNK) == column
    order = jnp.where(order, 1.0, 0.0).astype(BF16)
    for b in range(SLOTS // CHUNK):
        moved = dot(order, got_ref[b * TILE : (b + 1) * TILE]).astype(BF16)
        for k in range(FOLD):
            rows_ref[b * CHUNK : (b + 1) * CHUNK, k * WIDTH : (k + 1) * WIDTH] = moved[
                k * CHUNK : (k + 1) * CHUNK
            ]


def hidden_kernel(rows_ref, gate_ref, up_ref, hidden_ref):
    gate = dot(rows_ref[...], gate_ref[...])
    up = dot(rows_ref[...], up_ref[...])
    hidden_ref[...] = (jax.nn.silu(gate) * up).astype(BF16)


def down_kernel(own_ref, other_ref, own_down, other_down, made_ref, parts):
    for k in range(0, FOLD, 2):
        columns = slice(k * WIDTH, (k + 2) * WIDTH)
        made = dot(own_ref[...], own_down[:, columns]) + dot(other_ref[...], other_down[:, columns])
        made = made.astype(BF16)
        parts[k], parts[k + 1] = made[:, :WIDTH], made[:, WIDTH:]
    row, column = index_of((TILE, TILE), 0), index_of((TILE, TILE), 1)
    order = remainder(row, FOLD) * CHUNK + quotient(row, FOLD) == column
    order = jnp.where(order, 1.0, 0.0).astype(BF16)
    for b in range(SLOTS // CHUNK):
        rows = [parts[k, b * CHUNK : (b + 1) * CHUNK] for k in range(FOLD)]
        moved = dot(order, jnp.concatenate(rows, axis=0))
        made_ref[b * TILE : (b + 1) * TILE] = moved.astype(BF16)


def combine_kernel(mix_ref, got_ref, out_ref):
    half = CELLS * MESSAGE
    total = jnp.zeros((FOLD * ROWS, WIDTH), F32)
    for y in range(4):
        total = total + dot(mix_ref[:, y // 2 * half : (y // 2 + 1) * half], got_ref[y])
    total = total.astype(BF16)
    for k in range(FOLD):
        out_ref[:, k * WIDTH : (k + 1) * WIDTH] = total[k * ROWS : (k + 1) * ROWS]


def place_of(z, x, y, c):
    return ((z * 4 + x) * 4 + y) * 2 + c


ORDER = (3, 2, 1, 0)
SAME_CORE = [[place_of(z, x, y, c) for y in ORDER for z in ORDER for x in ORDER] for c in range(2)]


def exchange(values):
    values = values.reshape(SENDERS, MESSAGE, WIDTH)
    return lax.all_to_all(
        values, ALL, split_axis=0, concat_axis=0, axis_index_groups=SAME_CORE, tiled=True
    )


def swap_cores(values):
    return lax.ppermute(values, ALL, [(i, i ^ 1) for i in range(2 * SENDERS)])


def cost(flops, size):
    return pl.CostEstimate(flops=flops, bytes_accessed=size, transcendentals=0)


def expert_rows(
    attention, expert_input, expert_ids, route_gates, gate_weight, up_weight, down_weight
):
    ids = jnp.pad(expert_ids.astype(BF16), ((0, 0), (D, META - TOP)))
    gates = jnp.pad(route_gates, ((0, 0), (D + TOP, META - 2 * TOP)))
    packed = jnp.pad(expert_input, ((0, 0), (0, META)))
    packed = packed + (ids + gates)
    send, mix = call(
        select_kernel, "select",
        (array(2, 2, CELLS * MESSAGE, WIDTH), array(FOLD * ROWS, 2 * CELLS * MESSAGE)),
        packed, cost_estimate=cost(8 * 10**9, 4 * SLOTS * D),
    )
    got = exchange(send).reshape(SLOTS * FOLD, WIDTH)
    down_other = swap_cores(down_weight)
    rows = call(
        unfold_kernel, "unfold", array(SLOTS, D), got, cost_estimate=cost(10**9, 4 * SLOTS * D)
    )
    rows_other = swap_cores(rows)
    queries, latent_cache, cache_lengths = attention
    queries, rows = lax.optimization_barrier((queries, rows))
    context = attention_rows(queries, latent_cache, cache_lengths)

    flops, size = 4 * SLOTS * D * HIDDEN, 4 * D * HIDDEN

    def hidden_rows(held):
        return call(
            hidden_kernel, "hidden", array(SLOTS, HIDDEN), held, gate_weight, up_weight,
            cost_estimate=cost(flops, size),
        )

    own, rows_other = lax.optimization_barrier((hidden_rows(rows), rows_other))
    other = swap_cores(hidden_rows(rows_other))
    context, other = lax.optimization_barrier((context, other))
    made = call(
        down_kernel, "down", array(SLOTS * FOLD, WIDTH),
        own, other, down_weight, down_other, cost_estimate=cost(flops, size),
        scratch_shapes=[pltpu.VMEM((FOLD, SLOTS, WIDTH), BF16)],
    )
    returned = exchange(made).reshape(4, CELLS * MESSAGE, WIDTH)
    return context, call(combine_kernel, "combine", array(ROWS, D), mix, returned)


def per_device(
    queries,
    latent_cache,
    cache_lengths,
    expert_input,
    expert_ids,
    route_gates,
    gate_weight,
    up_weight,
    down_weight,
):
    attention = (queries, latent_cache, cache_lengths)
    return expert_rows(
        attention, expert_input, expert_ids, route_gates, gate_weight, up_weight, down_weight
    )


def solution(mesh):
    chips = Mesh(mesh.devices.reshape(2 * SENDERS), (ALL,))
    return jax.shard_map(
        per_device,
        mesh=chips,
        in_specs=(
            P(ALL, None, None),
            P(ALL, None, None),
            P(ALL),
            P(ALL, None),
            P(ALL, None),
            P(ALL, None),
            P(None, ALL),
            P(None, ALL),
            P(ALL, None),
        ),
        out_specs=(P(ALL, None, None), P(ALL, None)),
        check_vma=False,
    )
```

```python
import jax
import jax.numpy as jnp
from jax import lax
from jax.experimental import pallas as pl
from jax.experimental.pallas import tpu as pltpu
from jax.sharding import Mesh, PartitionSpec as P

LAT = 512
ROPE = 64
NOPE = 128
EXPERTS = 32
TOP = 8
CAP = 3
D = 7168
HIDDEN = 512
ROWS = 8
FOLD = 8
WIDTH = D // FOLD
CELLS = 16
MESSAGE = CAP * FOLD
SENDERS = 64
SLOTS = SENDERS * CAP
CHUNK = 32
TILE = CHUNK * FOLD
ALL = "device"
BF16 = jnp.bfloat16
F32 = jnp.float32


def attention_rows(queries, latent_cache, cache_lengths):
    scores = jnp.einsum(
        "rhq,rjq->rhj", queries, latent_cache, preferred_element_type=F32
    ) * (NOPE + ROPE) ** (-0.5)
    positions = jnp.arange(latent_cache.shape[1], dtype=jnp.int32)
    visible = (positions[None, :] < cache_lengths[:, None])[:, None, :]
    highest = jnp.max(jnp.where(visible, scores, -jnp.inf), axis=2, keepdims=True)
    powers = jnp.where(visible, jnp.exp(scores - highest), 0.0)
    attention_weights = (powers / jnp.sum(powers, axis=2, keepdims=True)).astype(BF16)
    latents = latent_cache[:, :, :LAT]
    return jnp.einsum(
        "rhj,rjl->rhl", attention_weights, latents, preferred_element_type=F32
    ).astype(BF16)


def dot(a, b, contract=((1,), (0,))):
    return lax.dot_general(a, b, (contract, ((), ())), preferred_element_type=F32)


def array(*shape, dtype=BF16):
    return jax.ShapeDtypeStruct(shape, dtype)


def in_vmem(count):
    return [pl.BlockSpec(memory_space=pltpu.VMEM)] * count


def in_hbm(count):
    return [pl.BlockSpec(memory_space=pltpu.HBM)] * count


def call(kernel, name, out_shape, *operands, limit=12, scalars=0, hbm=0, **settings):
    many = isinstance(out_shape, tuple)
    return pl.pallas_call(
        kernel,
        in_specs=[pl.BlockSpec(memory_space=pltpu.SMEM)] * scalars
        + in_vmem(len(operands) - scalars - hbm)
        + in_hbm(hbm),
        out_specs=tuple(in_vmem(len(out_shape))) if many else in_vmem(1)[0],
        out_shape=out_shape,
        compiler_params=pltpu.CompilerParams(vmem_limit_bytes=limit << 20),
        name=name,
        **settings,
    )(*operands)


def index_of(shape, axis):
    return lax.broadcasted_iota(jnp.int32, shape, axis).astype(F32)


def quotient(values, divisor):
    return jnp.floor((values + 0.5) * (1.0 / divisor))


def remainder(values, divisor):
    return values - quotient(values, divisor) * divisor


def wanted_places(shape, axis):
    q, p = index_of(shape, axis), index_of(shape, 1 - axis)
    place = quotient(remainder(q, MESSAGE), FOLD)
    return jnp.where(remainder(q, FOLD) == quotient(p, ROWS), place, -2.0)


def tables_kernel(lanes_ref, wanted_ref, wanted_t_ref):
    q = index_of(lanes_ref.shape, 0)
    h = quotient(q, CELLS * MESSAGE)
    expert = (EXPERTS - 1) - (quotient(q - h * (CELLS * MESSAGE), MESSAGE) * 2 + h)
    lanes_ref[...] = jnp.where(expert == index_of(lanes_ref.shape, 1), 1.0, 0.0).astype(BF16)
    wanted_ref[...] = wanted_places(wanted_ref.shape, 0)
    wanted_t_ref[...] = wanted_places(wanted_t_ref.shape, 1)


def select_kernel(
    input_ref, ids_ref, gates_ref, lanes_ref, wanted_ref, wanted_t_ref, send_ref, mix_ref
):
    ids, gates = ids_ref[...].astype(F32), gates_ref[...].astype(F32)
    lane = index_of((ROWS, EXPERTS), 1)
    member = jnp.zeros(lane.shape, F32)
    gate = jnp.zeros(lane.shape, F32)
    for k in range(TOP):
        hit = ids[:, k : k + 1] == lane
        member = member + jnp.where(hit, 1.0, 0.0)
        gate = gate + jnp.where(hit, gates[:, k : k + 1], 0.0)
    earlier = index_of((ROWS, ROWS), 1) < index_of((ROWS, ROWS), 0)
    rank = dot(jnp.where(earlier, 1.0, 0.0), member)
    place = jnp.where(member > 0.0, rank, -1.0)
    place = jnp.concatenate([place] * FOLD, axis=0).astype(BF16)
    gate = jnp.concatenate([gate] * FOLD, axis=0).astype(BF16)
    folded = jnp.concatenate(
        [input_ref[:, k * WIDTH : (k + 1) * WIDTH] for k in range(FOLD)], axis=0
    )
    half = CELLS * MESSAGE
    lanes = lanes_ref[...]
    chosen = dot(lanes, place, ((1,), (1,))) == wanted_ref[...]
    pick = jnp.where(chosen, 1.0, 0.0).astype(BF16)
    for h in range(2):
        picked = dot(pick[h * half : (h + 1) * half], folded).astype(BF16)
        send_ref[h, 0] = picked
        send_ref[h, 1] = picked

    chosen = dot(place, lanes, ((1,), (1,))) == wanted_t_ref[...]
    weight = dot(gate, lanes, ((1,), (1,)))
    mix_ref[...] = jnp.where(chosen, weight, 0.0).astype(BF16)


def unfold_kernel(got_ref, rows_ref):
    row, column = index_of((TILE, TILE), 0), index_of((TILE, TILE), 1)
    order = remainder(row, CHUNK) * FOLD + quotient(row, CHUNK) == column
    order = jnp.where(order, 1.0, 0.0).astype(BF16)
    for b in range(SLOTS // CHUNK):
        moved = dot(order, got_ref[b * TILE : (b + 1) * TILE]).astype(BF16)
        for k in range(FOLD):
            rows_ref[b * CHUNK : (b + 1) * CHUNK, k * WIDTH : (k + 1) * WIDTH] = moved[
                k * CHUNK : (k + 1) * CHUNK
            ]


def hidden_kernel(rows_ref, gate_ref, up_ref, hidden_ref):
    gate = dot(rows_ref[...], gate_ref[...])
    up = dot(rows_ref[...], up_ref[...])
    hidden_ref[...] = (jax.nn.silu(gate) * up).astype(BF16)


def down_kernel(own_ref, other_ref, own_down, other_down, made_ref, parts):
    for k in range(0, FOLD, 2):
        columns = slice(k * WIDTH, (k + 2) * WIDTH)
        made = dot(own_ref[...], own_down[:, columns]) + dot(other_ref[...], other_down[:, columns])
        made = made.astype(BF16)
        parts[k], parts[k + 1] = made[:, :WIDTH], made[:, WIDTH:]
    row, column = index_of((TILE, TILE), 0), index_of((TILE, TILE), 1)
    order = remainder(row, FOLD) * CHUNK + quotient(row, FOLD) == column
    order = jnp.where(order, 1.0, 0.0).astype(BF16)
    for b in range(SLOTS // CHUNK):
        rows = [parts[k, b * CHUNK : (b + 1) * CHUNK] for k in range(FOLD)]
        moved = dot(order, jnp.concatenate(rows, axis=0))
        made_ref[b * TILE : (b + 1) * TILE] = moved.astype(BF16)


def combine_kernel(mix_ref, got_ref, out_ref):
    half = CELLS * MESSAGE
    total = jnp.zeros((FOLD * ROWS, WIDTH), F32)
    for y in range(4):
        total = total + dot(mix_ref[:, y // 2 * half : (y // 2 + 1) * half], got_ref[y])
    total = total.astype(BF16)
    for k in range(FOLD):
        out_ref[:, k * WIDTH : (k + 1) * WIDTH] = total[k * ROWS : (k + 1) * ROWS]


def place_of(z, x, y, c):
    return ((z * 4 + x) * 4 + y) * 2 + c


ORDER = (3, 2, 1, 0)
SAME_CORE = [[place_of(z, x, y, c) for y in ORDER for z in ORDER for x in ORDER] for c in range(2)]


def exchange(values):
    values = values.reshape(SENDERS, MESSAGE, WIDTH)
    return lax.all_to_all(
        values, ALL, split_axis=0, concat_axis=0, axis_index_groups=SAME_CORE, tiled=True
    )


def swap_cores(values):
    return lax.ppermute(values, ALL, [(i, i ^ 1) for i in range(2 * SENDERS)])


def cost(flops, size):
    return pl.CostEstimate(flops=flops, bytes_accessed=size, transcendentals=0)


def expert_rows(
    attention, expert_input, expert_ids, route_gates, gate_weight, up_weight, down_weight
):
    slots, shared = 2 * CELLS * MESSAGE, FOLD * ROWS
    tables = call(
        tables_kernel, "tables",
        (array(slots, EXPERTS), array(slots, shared, dtype=F32), array(shared, slots, dtype=F32)),
        cost_estimate=cost(8 * 10**9, 4 * SLOTS * D),
    )
    send, mix = call(
        select_kernel, "select", (array(2, 2, CELLS * MESSAGE, WIDTH), array(shared, slots)),
        expert_input, expert_ids, route_gates, *tables,
        cost_estimate=cost(8 * 10**9, 4 * SLOTS * D),
    )
    got = exchange(send).reshape(SLOTS * FOLD, WIDTH)
    down_other = swap_cores(down_weight)
    rows = call(
        unfold_kernel, "unfold", array(SLOTS, D), got, cost_estimate=cost(10**9, 4 * SLOTS * D)
    )
    rows_other = swap_cores(rows)
    queries, latent_cache, cache_lengths = attention
    queries, rows = lax.optimization_barrier((queries, rows))
    context = attention_rows(queries, latent_cache, cache_lengths)

    flops, size = 4 * SLOTS * D * HIDDEN, 4 * D * HIDDEN

    def hidden_rows(held):
        return call(
            hidden_kernel, "hidden", array(SLOTS, HIDDEN), held, gate_weight, up_weight,
            cost_estimate=cost(flops, size),
        )

    own, rows_other = lax.optimization_barrier((hidden_rows(rows), rows_other))
    other = swap_cores(hidden_rows(rows_other))
    context, other = lax.optimization_barrier((context, other))
    made = call(
        down_kernel, "down", array(SLOTS * FOLD, WIDTH),
        own, other, down_weight, down_other, cost_estimate=cost(flops, size),
        scratch_shapes=[pltpu.VMEM((FOLD, SLOTS, WIDTH), BF16)],
    )
    returned = exchange(made).reshape(4, CELLS * MESSAGE, WIDTH)
    return context, call(combine_kernel, "combine", array(ROWS, D), mix, returned)


def per_device(
    queries,
    latent_cache,
    cache_lengths,
    expert_input,
    expert_ids,
    route_gates,
    gate_weight,
    up_weight,
    down_weight,
):
    attention = (queries, latent_cache, cache_lengths)
    return expert_rows(
        attention, expert_input, expert_ids, route_gates, gate_weight, up_weight, down_weight
    )


def solution(mesh):
    chips = Mesh(mesh.devices.reshape(2 * SENDERS), (ALL,))
    return jax.shard_map(
        per_device,
        mesh=chips,
        in_specs=(
            P(ALL, None, None),
            P(ALL, None, None),
            P(ALL),
            P(ALL, None),
            P(ALL, None),
            P(ALL, None),
            P(None, ALL),
            P(None, ALL),
            P(ALL, None),
        ),
        out_specs=(P(ALL, None, None), P(ALL, None)),
        check_vma=False,
    )
```

```python
import jax
import jax.numpy as jnp
from jax import lax
from jax.experimental import pallas as pl
from jax.experimental.pallas import tpu as pltpu
from jax.sharding import Mesh, PartitionSpec as P

LAT = 512
ROPE = 64
NOPE = 128
EXPERTS = 32
TOP = 8
CAP = 3
D = 7168
HIDDEN = 512
ROWS = 8
FOLD = 8
WIDTH = D // FOLD
CELLS = 16
MESSAGE = CAP * FOLD
SENDERS = 64
SLOTS = SENDERS * CAP
CHUNK = 32
TILE = CHUNK * FOLD
ALL = "device"
BF16 = jnp.bfloat16
F32 = jnp.float32


def attention_rows(queries, latent_cache, cache_lengths):
    scores = jnp.einsum(
        "rhq,rjq->rhj", queries, latent_cache, preferred_element_type=F32
    ) * (NOPE + ROPE) ** (-0.5)
    positions = jnp.arange(latent_cache.shape[1], dtype=jnp.int32)
    visible = (positions[None, :] < cache_lengths[:, None])[:, None, :]
    highest = jnp.max(jnp.where(visible, scores, -jnp.inf), axis=2, keepdims=True)
    powers = jnp.where(visible, jnp.exp(scores - highest), 0.0)
    attention_weights = (powers / jnp.sum(powers, axis=2, keepdims=True)).astype(BF16)
    latents = latent_cache[:, :, :LAT]
    return jnp.einsum(
        "rhj,rjl->rhl", attention_weights, latents, preferred_element_type=F32
    ).astype(BF16)


def dot(a, b, contract=((1,), (0,))):
    return lax.dot_general(a, b, (contract, ((), ())), preferred_element_type=F32)


def array(*shape, dtype=BF16):
    return jax.ShapeDtypeStruct(shape, dtype)


def in_vmem(count):
    return [pl.BlockSpec(memory_space=pltpu.VMEM)] * count


def in_hbm(count):
    return [pl.BlockSpec(memory_space=pltpu.HBM)] * count


def call(kernel, name, out_shape, *operands, limit=12, scalars=0, hbm=0, **settings):
    many = isinstance(out_shape, tuple)
    return pl.pallas_call(
        kernel,
        in_specs=[pl.BlockSpec(memory_space=pltpu.SMEM)] * scalars
        + in_vmem(len(operands) - scalars - hbm)
        + in_hbm(hbm),
        out_specs=tuple(in_vmem(len(out_shape))) if many else in_vmem(1)[0],
        out_shape=out_shape,
        compiler_params=pltpu.CompilerParams(vmem_limit_bytes=limit << 20),
        name=name,
        **settings,
    )(*operands)


def index_of(shape, axis):
    return lax.broadcasted_iota(jnp.int32, shape, axis).astype(F32)


def quotient(values, divisor):
    return jnp.floor((values + 0.5) * (1.0 / divisor))


def remainder(values, divisor):
    return values - quotient(values, divisor) * divisor


def wanted_places(shape, axis):
    q, p = index_of(shape, axis), index_of(shape, 1 - axis)
    place = quotient(remainder(q, MESSAGE), FOLD)
    return jnp.where(remainder(q, FOLD) == quotient(p, ROWS), place, -2.0)


def tables_kernel(lanes_ref, wanted_ref, wanted_t_ref):
    q = index_of(lanes_ref.shape, 0)
    h = quotient(q, CELLS * MESSAGE)
    expert = (EXPERTS - 1) - (quotient(q - h * (CELLS * MESSAGE), MESSAGE) * 2 + h)
    lanes_ref[...] = jnp.where(expert == index_of(lanes_ref.shape, 1), 1.0, 0.0).astype(BF16)
    wanted_ref[...] = wanted_places(wanted_ref.shape, 0)
    wanted_t_ref[...] = wanted_places(wanted_t_ref.shape, 1)


def select_kernel(
    input_ref, ids_ref, gates_ref, lanes_ref, wanted_ref, wanted_t_ref, send_ref, mix_ref
):
    ids, gates = ids_ref[...].astype(F32), gates_ref[...].astype(F32)
    lane = index_of((ROWS, EXPERTS), 1)
    member = jnp.zeros(lane.shape, F32)
    gate = jnp.zeros(lane.shape, F32)
    for k in range(TOP):
        hit = ids[:, k : k + 1] == lane
        member = member + jnp.where(hit, 1.0, 0.0)
        gate = gate + jnp.where(hit, gates[:, k : k + 1], 0.0)
    earlier = index_of((ROWS, ROWS), 1) < index_of((ROWS, ROWS), 0)
    rank = dot(jnp.where(earlier, 1.0, 0.0), member)
    place = jnp.where(member > 0.0, rank, -1.0)
    place = jnp.concatenate([place] * FOLD, axis=0).astype(BF16)
    gate = jnp.concatenate([gate] * FOLD, axis=0).astype(BF16)
    folded = jnp.concatenate(
        [input_ref[:, k * WIDTH : (k + 1) * WIDTH] for k in range(FOLD)], axis=0
    )
    half = CELLS * MESSAGE
    lanes = lanes_ref[...]
    chosen = dot(lanes, place, ((1,), (1,))) == wanted_ref[...]
    pick = jnp.where(chosen, 1.0, 0.0).astype(BF16)
    for h in range(2):
        picked = dot(pick[h * half : (h + 1) * half], folded).astype(BF16)
        send_ref[h, 0] = picked
        send_ref[h, 1] = picked

    chosen = dot(place, lanes, ((1,), (1,))) == wanted_t_ref[...]
    weight = dot(gate, lanes, ((1,), (1,)))
    mix_ref[...] = jnp.where(chosen, weight, 0.0).astype(BF16)


def unfold(got_ref, rows_ref):
    row, column = index_of((TILE, TILE), 0), index_of((TILE, TILE), 1)
    order = remainder(row, CHUNK) * FOLD + quotient(row, CHUNK) == column
    order = jnp.where(order, 1.0, 0.0).astype(BF16)
    for b in range(SLOTS // CHUNK):
        moved = dot(order, got_ref[b * TILE : (b + 1) * TILE]).astype(BF16)
        for k in range(FOLD):
            rows_ref[b * CHUNK : (b + 1) * CHUNK, k * WIDTH : (k + 1) * WIDTH] = moved[
                k * CHUNK : (k + 1) * CHUNK
            ]


def hidden_kernel(got_ref, gate_ref, up_ref, hidden_ref, rows):
    unfold(got_ref, rows)
    gate = dot(rows[...], gate_ref[...])
    up = dot(rows[...], up_ref[...])
    hidden_ref[...] = (jax.nn.silu(gate) * up).astype(BF16)


def down_kernel(own_ref, other_ref, own_down, other_down, made_ref, parts):
    for k in range(0, FOLD, 2):
        columns = slice(k * WIDTH, (k + 2) * WIDTH)
        made = dot(own_ref[...], own_down[:, columns]) + dot(other_ref[...], other_down[:, columns])
        made = made.astype(BF16)
        parts[k], parts[k + 1] = made[:, :WIDTH], made[:, WIDTH:]
    row, column = index_of((TILE, TILE), 0), index_of((TILE, TILE), 1)
    order = remainder(row, FOLD) * CHUNK + quotient(row, FOLD) == column
    order = jnp.where(order, 1.0, 0.0).astype(BF16)
    for b in range(SLOTS // CHUNK):
        rows = [parts[k, b * CHUNK : (b + 1) * CHUNK] for k in range(FOLD)]
        moved = dot(order, jnp.concatenate(rows, axis=0))
        made_ref[b * TILE : (b + 1) * TILE] = moved.astype(BF16)


def combine_kernel(mix_ref, got_ref, out_ref):
    half = CELLS * MESSAGE
    total = jnp.zeros((FOLD * ROWS, WIDTH), F32)
    for y in range(4):
        total = total + dot(mix_ref[:, y // 2 * half : (y // 2 + 1) * half], got_ref[y])
    total = total.astype(BF16)
    for k in range(FOLD):
        out_ref[:, k * WIDTH : (k + 1) * WIDTH] = total[k * ROWS : (k + 1) * ROWS]


def place_of(z, x, y, c):
    return ((z * 4 + x) * 4 + y) * 2 + c


ORDER = (3, 2, 1, 0)
SAME_CORE = [[place_of(z, x, y, c) for y in ORDER for z in ORDER for x in ORDER] for c in range(2)]


def exchange(values):
    values = values.reshape(SENDERS, MESSAGE, WIDTH)
    return lax.all_to_all(
        values, ALL, split_axis=0, concat_axis=0, axis_index_groups=SAME_CORE, tiled=True
    )


def swap_cores(values):
    return lax.ppermute(values, ALL, [(i, i ^ 1) for i in range(2 * SENDERS)])


def cost(flops, size):
    return pl.CostEstimate(flops=flops, bytes_accessed=size, transcendentals=0)


def expert_rows(
    attention, expert_input, expert_ids, route_gates, gate_weight, up_weight, down_weight
):
    slots, shared = 2 * CELLS * MESSAGE, FOLD * ROWS
    tables = call(
        tables_kernel, "tables",
        (array(slots, EXPERTS), array(slots, shared, dtype=F32), array(shared, slots, dtype=F32)),
        cost_estimate=cost(8 * 10**9, 4 * SLOTS * D),
    )
    send, mix = call(
        select_kernel, "select", (array(2, 2, CELLS * MESSAGE, WIDTH), array(shared, slots)),
        expert_input, expert_ids, route_gates, *tables,
        cost_estimate=cost(8 * 10**9, 4 * SLOTS * D),
    )
    got = exchange(send).reshape(SLOTS * FOLD, WIDTH)
    down_other = swap_cores(down_weight)
    got_other = swap_cores(got)
    queries, latent_cache, cache_lengths = attention
    queries, got = lax.optimization_barrier((queries, got))
    context = attention_rows(queries, latent_cache, cache_lengths)

    flops, size = 4 * SLOTS * D * HIDDEN, 4 * D * HIDDEN

    def hidden_rows(held):
        return call(
            hidden_kernel, "hidden", array(SLOTS, HIDDEN), held, gate_weight, up_weight,
            cost_estimate=cost(flops, size), scratch_shapes=[pltpu.VMEM((SLOTS, D), BF16)],
        )

    own, got_other = lax.optimization_barrier((hidden_rows(got), got_other))
    other = swap_cores(hidden_rows(got_other))
    context, other = lax.optimization_barrier((context, other))
    made = call(
        down_kernel, "down", array(SLOTS * FOLD, WIDTH),
        own, other, down_weight, down_other, cost_estimate=cost(flops, size),
        scratch_shapes=[pltpu.VMEM((FOLD, SLOTS, WIDTH), BF16)],
    )
    returned = exchange(made).reshape(4, CELLS * MESSAGE, WIDTH)
    return context, call(combine_kernel, "combine", array(ROWS, D), mix, returned)


def per_device(
    queries,
    latent_cache,
    cache_lengths,
    expert_input,
    expert_ids,
    route_gates,
    gate_weight,
    up_weight,
    down_weight,
):
    attention = (queries, latent_cache, cache_lengths)
    return expert_rows(
        attention, expert_input, expert_ids, route_gates, gate_weight, up_weight, down_weight
    )


def solution(mesh):
    chips = Mesh(mesh.devices.reshape(2 * SENDERS), (ALL,))
    return jax.shard_map(
        per_device,
        mesh=chips,
        in_specs=(
            P(ALL, None, None),
            P(ALL, None, None),
            P(ALL),
            P(ALL, None),
            P(ALL, None),
            P(ALL, None),
            P(None, ALL),
            P(None, ALL),
            P(ALL, None),
        ),
        out_specs=(P(ALL, None, None), P(ALL, None)),
        check_vma=False,
    )
```

```python
import jax
import jax.numpy as jnp
from jax import lax
from jax.experimental import pallas as pl
from jax.experimental.pallas import tpu as pltpu
from jax.sharding import Mesh, PartitionSpec as P

LAT = 512
ROPE = 64
NOPE = 128
EXPERTS = 32
TOP = 8
CAP = 3
D = 7168
HIDDEN = 512
ROWS = 8
FOLD = 8
WIDTH = D // FOLD
CELLS = 16
MESSAGE = CAP * FOLD
SENDERS = 64
SLOTS = SENDERS * CAP
CHUNK = 32
TILE = CHUNK * FOLD
ALL = "device"
BF16 = jnp.bfloat16
F32 = jnp.float32


def attention_rows(queries, latent_cache, cache_lengths):
    scores = jnp.einsum(
        "rhq,rjq->rhj", queries, latent_cache, preferred_element_type=F32
    ) * (NOPE + ROPE) ** (-0.5)
    positions = jnp.arange(latent_cache.shape[1], dtype=jnp.int32)
    visible = (positions[None, :] < cache_lengths[:, None])[:, None, :]
    highest = jnp.max(jnp.where(visible, scores, -jnp.inf), axis=2, keepdims=True)
    powers = jnp.where(visible, jnp.exp(scores - highest), 0.0)
    latents = latent_cache[:, :, :LAT]
    summed = jnp.einsum(
        "rhj,rjl->rhl", powers.astype(BF16), latents, preferred_element_type=F32
    )
    return (summed / jnp.sum(powers, axis=2, keepdims=True)).astype(BF16)


def dot(a, b, contract=((1,), (0,))):
    return lax.dot_general(a, b, (contract, ((), ())), preferred_element_type=F32)


def array(*shape, dtype=BF16):
    return jax.ShapeDtypeStruct(shape, dtype)


def in_vmem(count):
    return [pl.BlockSpec(memory_space=pltpu.VMEM)] * count


def in_hbm(count):
    return [pl.BlockSpec(memory_space=pltpu.HBM)] * count


def call(kernel, name, out_shape, *operands, limit=12, scalars=0, hbm=0, **settings):
    many = isinstance(out_shape, tuple)
    return pl.pallas_call(
        kernel,
        in_specs=[pl.BlockSpec(memory_space=pltpu.SMEM)] * scalars
        + in_vmem(len(operands) - scalars - hbm)
        + in_hbm(hbm),
        out_specs=tuple(in_vmem(len(out_shape))) if many else in_vmem(1)[0],
        out_shape=out_shape,
        compiler_params=pltpu.CompilerParams(vmem_limit_bytes=limit << 20),
        name=name,
        **settings,
    )(*operands)


def index_of(shape, axis):
    return lax.broadcasted_iota(jnp.int32, shape, axis).astype(F32)


def quotient(values, divisor):
    return jnp.floor((values + 0.5) * (1.0 / divisor))


def remainder(values, divisor):
    return values - quotient(values, divisor) * divisor


def wanted_places(shape, axis):
    q, p = index_of(shape, axis), index_of(shape, 1 - axis)
    place = quotient(remainder(q, MESSAGE), FOLD)
    return jnp.where(remainder(q, FOLD) == quotient(p, ROWS), place, -2.0)


def tables_kernel(lanes_ref, wanted_ref, wanted_t_ref):
    q = index_of(lanes_ref.shape, 0)
    h = quotient(q, CELLS * MESSAGE)
    expert = (EXPERTS - 1) - (quotient(q - h * (CELLS * MESSAGE), MESSAGE) * 2 + h)
    lanes_ref[...] = jnp.where(expert == index_of(lanes_ref.shape, 1), 1.0, 0.0).astype(BF16)
    wanted_ref[...] = wanted_places(wanted_ref.shape, 0)
    wanted_t_ref[...] = wanted_places(wanted_t_ref.shape, 1)


def pick_kernel(ids_ref, gates_ref, lanes_ref, wanted_ref, wanted_t_ref, pick_ref, mix_ref):
    ids, gates = ids_ref[...].astype(F32), gates_ref[...].astype(F32)
    lane = index_of((ROWS, EXPERTS), 1)
    member = jnp.zeros(lane.shape, F32)
    gate = jnp.zeros(lane.shape, F32)
    for k in range(TOP):
        hit = ids[:, k : k + 1] == lane
        member = member + jnp.where(hit, 1.0, 0.0)
        gate = gate + jnp.where(hit, gates[:, k : k + 1], 0.0)
    earlier = index_of((ROWS, ROWS), 1) < index_of((ROWS, ROWS), 0)
    rank = dot(jnp.where(earlier, 1.0, 0.0), member)
    place = jnp.where(member > 0.0, rank, -1.0)
    place = jnp.concatenate([place] * FOLD, axis=0).astype(BF16)
    gate = jnp.concatenate([gate] * FOLD, axis=0).astype(BF16)
    lanes = lanes_ref[...]
    chosen = dot(lanes, place, ((1,), (1,))) == wanted_ref[...]
    pick_ref[...] = jnp.where(chosen, 1.0, 0.0).astype(BF16)
    chosen = dot(place, lanes, ((1,), (1,))) == wanted_t_ref[...]
    weight = dot(gate, lanes, ((1,), (1,)))
    mix_ref[...] = jnp.where(chosen, weight, 0.0).astype(BF16)


def select_kernel(input_ref, pick_ref, send_ref):
    folded = jnp.concatenate(
        [input_ref[:, k * WIDTH : (k + 1) * WIDTH] for k in range(FOLD)], axis=0
    )
    half = CELLS * MESSAGE
    for h in range(2):
        picked = dot(pick_ref[h * half : (h + 1) * half], folded).astype(BF16)
        send_ref[h, 0] = picked
        send_ref[h, 1] = picked


def unfold(got_ref, rows_ref):
    row, column = index_of((TILE, TILE), 0), index_of((TILE, TILE), 1)
    order = remainder(row, CHUNK) * FOLD + quotient(row, CHUNK) == column
    order = jnp.where(order, 1.0, 0.0).astype(BF16)
    for b in range(SLOTS // CHUNK):
        moved = dot(order, got_ref[b * TILE : (b + 1) * TILE]).astype(BF16)
        for k in range(FOLD):
            rows_ref[b * CHUNK : (b + 1) * CHUNK, k * WIDTH : (k + 1) * WIDTH] = moved[
                k * CHUNK : (k + 1) * CHUNK
            ]


def hidden_kernel(got_ref, gate_ref, up_ref, hidden_ref, rows):
    unfold(got_ref, rows)
    gate = dot(rows[...], gate_ref[...])
    up = dot(rows[...], up_ref[...])
    hidden_ref[...] = (jax.nn.silu(gate) * up).astype(BF16)


def down_kernel(own_ref, other_ref, own_down, other_down, made_ref, parts):
    for k in range(0, FOLD, 2):
        columns = slice(k * WIDTH, (k + 2) * WIDTH)
        made = dot(own_ref[...], own_down[:, columns]) + dot(other_ref[...], other_down[:, columns])
        made = made.astype(BF16)
        parts[k], parts[k + 1] = made[:, :WIDTH], made[:, WIDTH:]
    row, column = index_of((TILE, TILE), 0), index_of((TILE, TILE), 1)
    order = remainder(row, FOLD) * CHUNK + quotient(row, FOLD) == column
    order = jnp.where(order, 1.0, 0.0).astype(BF16)
    for b in range(SLOTS // CHUNK):
        rows = [parts[k, b * CHUNK : (b + 1) * CHUNK] for k in range(FOLD)]
        moved = dot(order, jnp.concatenate(rows, axis=0))
        made_ref[b * TILE : (b + 1) * TILE] = moved.astype(BF16)


def combine_kernel(mix_ref, got_ref, out_ref):
    half = CELLS * MESSAGE
    total = jnp.zeros((FOLD * ROWS, WIDTH), F32)
    for y in range(4):
        total = total + dot(mix_ref[:, y // 2 * half : (y // 2 + 1) * half], got_ref[y])
    total = total.astype(BF16)
    for k in range(FOLD):
        out_ref[:, k * WIDTH : (k + 1) * WIDTH] = total[k * ROWS : (k + 1) * ROWS]


def place_of(z, x, y, c):
    return ((z * 4 + x) * 4 + y) * 2 + c


ORDER = (3, 2, 1, 0)
SAME_CORE = [[place_of(z, x, y, c) for y in ORDER for z in ORDER for x in ORDER] for c in range(2)]


def exchange(values):
    values = values.reshape(SENDERS, MESSAGE, WIDTH)
    return lax.all_to_all(
        values, ALL, split_axis=0, concat_axis=0, axis_index_groups=SAME_CORE, tiled=True
    )


def swap_cores(values):
    return lax.ppermute(values, ALL, [(i, i ^ 1) for i in range(2 * SENDERS)])


def cost(flops, size):
    return pl.CostEstimate(flops=flops, bytes_accessed=size, transcendentals=0)


def expert_rows(
    attention, expert_input, expert_ids, route_gates, gate_weight, up_weight, down_weight
):
    slots, shared = 2 * CELLS * MESSAGE, FOLD * ROWS
    tables = call(
        tables_kernel, "tables",
        (array(slots, EXPERTS), array(slots, shared, dtype=F32), array(shared, slots, dtype=F32)),
        cost_estimate=cost(8 * 10**9, 4 * SLOTS * D),
    )
    pick, mix = call(
        pick_kernel, "pick", (array(slots, shared), array(shared, slots)),
        expert_ids, route_gates, *tables, cost_estimate=cost(2 * 10**9, 4 * SLOTS * D),
    )
    send = call(
        select_kernel, "select", array(2, 2, CELLS * MESSAGE, WIDTH), expert_input, pick,
        cost_estimate=cost(8 * 10**9, 4 * SLOTS * D),
    )
    got = exchange(send).reshape(SLOTS * FOLD, WIDTH)
    down_other = swap_cores(down_weight)
    got_other = swap_cores(got)
    queries, latent_cache, cache_lengths = attention
    queries, got = lax.optimization_barrier((queries, got))
    context = attention_rows(queries, latent_cache, cache_lengths)

    flops, size = 4 * SLOTS * D * HIDDEN, 4 * D * HIDDEN

    def hidden_rows(held):
        return call(
            hidden_kernel, "hidden", array(SLOTS, HIDDEN), held, gate_weight, up_weight,
            cost_estimate=cost(flops, size), scratch_shapes=[pltpu.VMEM((SLOTS, D), BF16)],
        )

    own, got_other = lax.optimization_barrier((hidden_rows(got), got_other))
    other = swap_cores(hidden_rows(got_other))
    context, other = lax.optimization_barrier((context, other))
    made = call(
        down_kernel, "down", array(SLOTS * FOLD, WIDTH),
        own, other, down_weight, down_other, cost_estimate=cost(flops, size),
        scratch_shapes=[pltpu.VMEM((FOLD, SLOTS, WIDTH), BF16)],
    )
    returned = exchange(made).reshape(4, CELLS * MESSAGE, WIDTH)
    return context, call(combine_kernel, "combine", array(ROWS, D), mix, returned)


def per_device(
    queries,
    latent_cache,
    cache_lengths,
    expert_input,
    expert_ids,
    route_gates,
    gate_weight,
    up_weight,
    down_weight,
):
    attention = (queries, latent_cache, cache_lengths)
    return expert_rows(
        attention, expert_input, expert_ids, route_gates, gate_weight, up_weight, down_weight
    )


def solution(mesh):
    chips = Mesh(mesh.devices.reshape(2 * SENDERS), (ALL,))
    return jax.shard_map(
        per_device,
        mesh=chips,
        in_specs=(
            P(ALL, None, None),
            P(ALL, None, None),
            P(ALL),
            P(ALL, None),
            P(ALL, None),
            P(ALL, None),
            P(None, ALL),
            P(None, ALL),
            P(ALL, None),
        ),
        out_specs=(P(ALL, None, None), P(ALL, None)),
        check_vma=False,
    )
```
